32 devices in a mesh: dp: 8 (over y, x, core), tensor: 4 (over z).
Axes of the slice: x: 2, y: 2, z: 4, core: 2. Of those that a mesh axis runs over, the one named last changes fastest.
Arguments:
- layer_input: bfloat16 [8192, 1024], P(('dp', 'tensor')), may hold values from -6 to 6
- lengths: int32 [8], P('dp'), may hold values from 769 to 1024, as said below
- input_gain: float32 [1024], replicated, may hold values from 0.5 to 1.5
- proj_gate: bfloat16 [1024, 2048], P('dp', 'tensor'), may hold values from -0.1875 to 0.1875
- proj_values: bfloat16 [1024, 2048], P('dp', 'tensor'), may hold values from -0.1875 to 0.1875
- proj_state: bfloat16 [1024, 256], P('dp'), may hold values from -0.1875 to 0.1875
- proj_step: bfloat16 [1024, 32], P('dp', 'tensor'), may hold values from -0.1875 to 0.1875
- conv_values: float32 [4, 2048], P(None, 'tensor'), may hold values from -3 to 3
- bias_values: float32 [2048], P('tensor'), may hold values from -3 to 3
- conv_state: float32 [4, 256], replicated, may hold values from -3 to 3
- bias_state: float32 [256], replicated, may hold values from -3 to 3
- step_bias: float32 [32], P('tensor'), may hold values from -6.9 to -2.3
- decay_log: float32 [32], P('tensor'), may hold values from 0 to 2.77
- skip_gain: float32 [32], P('tensor'), may hold values from 0.5 to 1.5
- mixer_gain: float32 [2048], P('tensor'), may hold values from 0.5 to 1.5
- proj_output: bfloat16 [1024, 2048], P('dp', 'tensor'), may hold values from -0.125 to 0.125
- out_grad: bfloat16 [8192, 1024], P(('dp', 'tensor')), may hold values from -6 to 6
Outputs:
- layer_output: bfloat16 [8192, 1024], P(('dp', 'tensor'))
- input_grad: bfloat16 [8192, 1024], P(('dp', 'tensor'))
- grad_input_gain: float32 [1024], replicated
- grad_proj_gate: float32 [1024, 2048], P('dp', 'tensor')
- grad_proj_values: float32 [1024, 2048], P('dp', 'tensor')
- grad_proj_state: float32 [1024, 256], P('dp')
- grad_proj_step: float32 [1024, 32], P('dp', 'tensor')
- grad_conv_values: float32 [4, 2048], P(None, 'tensor')
- grad_bias_values: float32 [2048], P('tensor')
- grad_conv_state: float32 [4, 256], replicated
- grad_bias_state: float32 [256], replicated
- grad_step_bias: float32 [32], P('tensor')
- grad_decay_log: float32 [32], P('tensor')
- grad_skip_gain: float32 [32], P('tensor')
- grad_mixer_gain: float32 [2048], P('tensor')
- grad_proj_output: float32 [1024, 2048], P('dp', 'tensor')
The draws below stay inside these ranges and needn't reach their ends.
Inputs may be any that keep to these rules, and one draw needn't show every extreme that they name: `lengths`: live slots of each group; its one sequence starts at the group's first slot and the rest is padding; some group is full in every draw.
All inputs are finite; a program needn't handle non-finite values.
Results may differ from the reference program's by a relative error of at most 0.015.
Values may be sent and summed in bfloat16 or wider, within the bound.
A program may use at most 128 MiB of HBM per device.

```python
from functools import partial
import jax
import jax.numpy as jnp
from jax import lax

D = 1024
HEADS = 32
STATE = 128
CONV = 4
BLOCK = 256
SEQ = 1024
INNER = 2048
TOKENS = 8192
N_DP = 8
N_TENSOR = 4


def draw_lengths(key, part):
    key = jax.random.fold_in(key, 11)
    key_lengths, key_full = jax.random.split(key)
    lowest = SEQ - SEQ // N_TENSOR + 1
    lengths_drawn = jax.random.randint(key_lengths, (N_DP,), lowest, SEQ + 1)
    full_group = jax.random.randint(key_full, (), 0, N_DP)
    return jnp.where(jnp.arange(N_DP) == full_group, SEQ, lengths_drawn).astype(jnp.int32)


def steps_of(stream_key, extent, shards, least, largest):
    def one(position, blocks):
        draws = jax.random.uniform(jax.random.fold_in(jax.random.fold_in(stream_key, 6), position), (blocks,), jnp.float32, least / len(shards), largest / len(shards))
        return jnp.repeat(jnp.exp(draws), extent[position] // blocks).reshape((-1,) + (1,) * (len(extent) - position - 1))

    factor_of = one(*shards[0])
    for cut in shards[1:]:
        factor_of = factor_of * one(*cut)
    return factor_of


def centred(stream_key, extent, deviation, most, cuts=(), held_as=jnp.bfloat16):
    drawn = jax.random.normal(stream_key, extent, jnp.float32) * deviation
    if len(cuts) > 0:
        drawn = steps_of(stream_key, extent, cuts, -0.22, 0.18) * drawn
    return jnp.clip(drawn, min=-most, max=most).astype(held_as)


def setup_inputs(seed: int = 0) -> dict:
    key_list = jax.random.split(jax.random.key(seed), 18)
    layer_input = centred(key_list[0], (TOKENS, D), 1.0, 6.0, ((0, 32),))
    lengths = draw_lengths(jax.random.fold_in(key_list[17], 71), 0)
    input_gain = jnp.clip(1.0 + 0.1 * jax.random.normal(key_list[2], (D,), jnp.float32), 0.5, 1.5)
    proj_gate = centred(key_list[3], (D, INNER), D ** -0.5, 0.1875, ((0, 8), (1, 4)))
    proj_values = centred(key_list[4], (D, INNER), D ** -0.5, 0.1875, ((0, 8), (1, 4)))
    proj_state = centred(key_list[5], (D, 2 * STATE), D ** -0.5, 0.1875, ((0, 8),))
    proj_step = centred(key_list[6], (D, HEADS), D ** -0.5, 0.1875, ((0, 8), (1, 4)))
    conv_values = centred(key_list[7], (CONV, INNER), CONV ** -0.5, 3.0, ((1, 4),), jnp.float32)
    bias_values = centred(key_list[8], (INNER,), 0.5, 3.0, ((0, 4),), jnp.float32)
    conv_state = centred(key_list[9], (CONV, 2 * STATE), CONV ** -0.5, 3.0, (), jnp.float32)
    bias_state = centred(key_list[10], (2 * STATE,), 0.5, 3.0, (), jnp.float32)
    step_bias = jnp.clip(-6.9 + 4.6000001430511475 * jax.random.uniform(key_list[11], (HEADS,), jnp.float32) ** steps_of(key_list[11], (HEADS,), ((0, 4),), -0.2, 0.2), -6.9, -2.3)
    decay_log = jnp.clip(2.77 * jax.random.uniform(key_list[12], (HEADS,), jnp.float32) ** steps_of(key_list[12], (HEADS,), ((0, 4),), -0.2, 0.2), 0.0, 2.77)
    skip_gain = jnp.clip(0.5 + 1.0 * jax.random.uniform(key_list[13], (HEADS,), jnp.float32) ** steps_of(key_list[13], (HEADS,), ((0, 4),), -0.2, 0.2), 0.5, 1.5)
    mixer_gain = jnp.clip(1.0 + 0.1 * jax.random.normal(key_list[14], (INNER,), jnp.float32), 0.5, 1.5)
    proj_output = centred(key_list[15], (D, INNER), INNER ** -0.5, 0.125, ((0, 8), (1, 4)))
    out_grad = centred(key_list[16], (TOKENS, D), 1.0, 6.0, ((0, 32),))
    return {"layer_input": layer_input, "lengths": lengths, "input_gain": input_gain, "proj_gate": proj_gate, "proj_values": proj_values, "proj_state": proj_state, "proj_step": proj_step, "conv_values": conv_values, "bias_values": bias_values, "conv_state": conv_state, "bias_state": bias_state, "step_bias": step_bias, "decay_log": decay_log, "skip_gain": skip_gain, "mixer_gain": mixer_gain, "proj_output": proj_output, "out_grad": out_grad}


HIGHEST = lax.Precision.HIGHEST
epsilon = 1e-05

@jax.custom_vjp
def low(v):
    return lax.optimization_barrier(v.astype(jnp.bfloat16)).astype(jnp.float32)

@jax.custom_vjp
def low_back(v):
    return v

def low_keep(v):
    return (low(v), None)

def low_pass(kept, grad):
    return (grad,)

def back_keep(v):
    return (v, None)

def back_low(kept, grad):
    return (low(grad),)
low.defvjp(low_keep, low_pass)
low_back.defvjp(back_keep, back_low)

def product(left_side, right_side):
    return jnp.dot(left_side, right_side, precision=HIGHEST)

def rms_scale(values, scale_gain):
    return values * lax.rsqrt(lax.optimization_barrier(jnp.mean(values * values, axis=-1, keepdims=True)) + epsilon) * scale_gain

def causal_conv(values, kernel, conv_shift):
    length = values.shape[0]
    padded = jnp.pad(values, ((CONV - 1, 0), (0, 0)))
    summed = conv_shift + jnp.zeros_like(values)
    for offset in range(CONV):
        summed = summed + kernel[offset] * padded[offset:offset + length]
    return summed

def block_scan(carry_state, pieces, decay_rate):
    values, step_sizes, input_map, output_map = pieces
    logdecay = jnp.cumsum(step_sizes * decay_rate, axis=0)
    spread = logdecay[:, None, :] - logdecay[None, :, :]
    causal = (jnp.arange(BLOCK)[:, None] >= jnp.arange(BLOCK)[None, :])[:, :, None]
    decays = jnp.exp(jnp.where(causal, spread, -10000.0))
    scores = jnp.dot(output_map, input_map.T, precision=HIGHEST)
    weights = low(scores[:, :, None] * decays)
    scaled = low(values * step_sizes[:, :, None])
    inside = jnp.einsum('ijh,jhp->ihp', weights, scaled, precision=HIGHEST)
    carried = jnp.einsum('in,hpn->ihp', output_map, carry_state, precision=HIGHEST) * jnp.exp(logdecay)[:, :, None]
    remain = jnp.exp(logdecay[-1][None, :] - logdecay)
    new_state = carry_state * jnp.exp(logdecay[-1])[:, None, None] + jnp.einsum('jhp,jn->hpn', scaled * remain[:, :, None], input_map, precision=HIGHEST)
    return (new_state, inside + carried)

def mixer_core(gate_in, values_in, state_in, step_in, conv_values, bias_values, conv_state, bias_state, step_bias, decay_log, skip_gain, present):
    length = values_in.shape[0]
    head_count = step_in.shape[1]
    head_dim = values_in.shape[1] // head_count
    state_width = state_in.shape[1] // 2
    values = low(jax.nn.silu(causal_conv(values_in, conv_values, bias_values)))
    state_maps = low(jax.nn.silu(causal_conv(state_in, conv_state, bias_state)))
    step_sizes = jax.nn.softplus(step_in + step_bias) * present[:, None]
    decay_rate = -jnp.exp(decay_log)
    blocks = length // BLOCK
    head_values = values.reshape(length, head_count, head_dim)
    pieces = (head_values.reshape(blocks, BLOCK, head_count, head_dim), step_sizes.reshape(blocks, BLOCK, head_count), state_maps[:, :state_width].reshape(blocks, BLOCK, state_width), state_maps[:, state_width:].reshape(blocks, BLOCK, state_width))
    initial = jnp.zeros((head_count, head_dim, state_width), jnp.float32)
    _, outputs = lax.scan(jax.checkpoint(partial(block_scan, decay_rate=decay_rate)), initial, pieces)
    mixed = outputs.reshape(length, head_count, head_dim) + skip_gain[None, :, None] * head_values
    mixed = mixed.reshape(length, head_count * head_dim) * present[:, None]
    return mixed * jax.nn.silu(gate_in)

def group_forward(rows_in, length, weights):
    input_gain, proj_gate, proj_values, proj_state, proj_step, conv_values, bias_values, conv_state, bias_state, step_bias, decay_log, skip_gain, mixer_gain, proj_output = weights
    present = (jnp.arange(SEQ) < length).astype(jnp.float32)
    normed = low(rms_scale(rows_in, input_gain))
    gate_in = low_back(product(normed, proj_gate))
    values_in = low_back(product(normed, proj_values))
    state_in = low_back(product(normed, proj_state))
    step_in = low_back(product(normed, proj_step))
    gated = mixer_core(gate_in, values_in, state_in, step_in, conv_values, bias_values, conv_state, bias_state, step_bias, decay_log, skip_gain, present)
    normed_out = low(rms_scale(gated, mixer_gain))
    return rows_in + jnp.dot(normed_out, proj_output.T, precision=HIGHEST)

def reference(layer_input, lengths, input_gain, proj_gate, proj_values, proj_state, proj_step, conv_values, bias_values, conv_state, bias_state, step_bias, decay_log, skip_gain, mixer_gain, proj_output, out_grad):
    groups = layer_input.astype(jnp.float32).reshape(N_DP, SEQ, D)
    weights = (input_gain, proj_gate.astype(jnp.float32), proj_values.astype(jnp.float32), proj_state.astype(jnp.float32), proj_step.astype(jnp.float32), conv_values, bias_values, conv_state, bias_state, step_bias, decay_log, skip_gain, mixer_gain, proj_output.astype(jnp.float32))

    def forward(group_rows, layer_weights):

        def one_group(group_pair):
            return group_forward(group_pair[0], group_pair[1], layer_weights)
        return lax.map(jax.checkpoint(one_group), (group_rows, lengths))
    outputs, pullback = jax.vjp(forward, groups, weights)
    grad_groups, gradients = pullback(out_grad.astype(jnp.float32).reshape(N_DP, SEQ, D))
    return (outputs.reshape(TOKENS, D).astype(jnp.bfloat16), grad_groups.reshape(TOKENS, D).astype(jnp.bfloat16), gradients[0], gradients[1], gradients[2], gradients[3], gradients[4], gradients[5], gradients[6], gradients[7], gradients[8], gradients[9], gradients[10], gradients[11], gradients[12], gradients[13])
```

```python
from functools import partial

import jax
import jax.numpy as jnp
from jax import lax
from jax.experimental import pallas as pl
from jax.experimental.pallas import tpu as pltpu
from jax.sharding import PartitionSpec as P

CONV = 4
BLOCK = 256
INNER = 2048


HIGHEST = lax.Precision.HIGHEST
epsilon = 1e-05


def rounded(v):
    return v + lax.stop_gradient(v.astype(jnp.bfloat16).astype(jnp.float32) - v)


def causal_conv(values, kernel, conv_shift):
    length = values.shape[0]
    padded = jnp.pad(values, ((CONV - 1, 0), (0, 0)))
    summed = conv_shift + jnp.zeros_like(values)
    for offset in range(CONV):
        summed = summed + kernel[offset] * padded[offset : offset + length]
    return summed


def block_scan(carry_state, pieces, decay_rate):
    values, step_sizes, input_map, output_map = pieces
    logdecay = jnp.cumsum(step_sizes * decay_rate, axis=0)
    spread = logdecay[:, None, :] - logdecay[None, :, :]
    causal = (jnp.arange(BLOCK)[:, None] >= jnp.arange(BLOCK)[None, :])[:, :, None]
    decays = jnp.exp(jnp.where(causal, spread, -10000.0))
    scores = jnp.dot(output_map, input_map.T, precision=HIGHEST)
    weights = rounded(scores[:, :, None] * decays)
    scaled = rounded(values * step_sizes[:, :, None])
    inside = jnp.einsum("ijh,jhp->ihp", weights, scaled, precision=HIGHEST)
    carried = (
        jnp.einsum("in,hpn->ihp", output_map, carry_state, precision=HIGHEST)
        * jnp.exp(logdecay)[:, :, None]
    )
    remain = jnp.exp(logdecay[-1][None, :] - logdecay)
    new_state = carry_state * jnp.exp(logdecay[-1])[:, None, None] + jnp.einsum(
        "jhp,jn->hpn", scaled * remain[:, :, None], input_map, precision=HIGHEST
    )
    return (new_state, inside + carried)


def mixer_core(
    gate_in,
    values_in,
    state_in,
    step_in,
    conv_values,
    bias_values,
    conv_state,
    bias_state,
    step_bias,
    decay_log,
    skip_gain,
    present,
):
    length = values_in.shape[0]
    head_count = step_in.shape[1]
    head_dim = values_in.shape[1] // head_count
    state_width = state_in.shape[1] // 2
    values = rounded(jax.nn.silu(causal_conv(values_in, conv_values, bias_values)))
    state_maps = rounded(jax.nn.silu(causal_conv(state_in, conv_state, bias_state)))
    step_sizes = jax.nn.softplus(step_in + step_bias) * present[:, None]
    decay_rate = -jnp.exp(decay_log)
    blocks = length // BLOCK
    head_values = values.reshape(length, head_count, head_dim)
    pieces = (
        head_values.reshape(blocks, BLOCK, head_count, head_dim),
        step_sizes.reshape(blocks, BLOCK, head_count),
        state_maps[:, :state_width].reshape(blocks, BLOCK, state_width),
        state_maps[:, state_width:].reshape(blocks, BLOCK, state_width),
    )
    initial = jnp.zeros((head_count, head_dim, state_width), jnp.float32)
    _, outputs = lax.scan(
        jax.checkpoint(partial(block_scan, decay_rate=decay_rate)), initial, pieces
    )
    mixed = outputs.reshape(length, head_count, head_dim) + skip_gain[None, :, None] * head_values
    mixed = mixed.reshape(length, head_count * head_dim) * present[:, None]
    return mixed * jax.nn.silu(gate_in)


def exchange_kernel(plan, sizes, *refs):
    count = len(plan)
    ins, outs = refs[:count], refs[count : 2 * count]
    slots = refs[2 * count : 3 * count]
    send_sem, recv_sem = refs[3 * count :]
    axes = sorted({axis for _, axis in plan})
    me = {axis: lax.axis_index(axis) for axis in axes}
    barrier = pltpu.get_barrier_semaphore()
    greeted = 0
    for axis in axes:
        size = sizes[axis]
        for step in range(1, size):
            peer = lax.rem(me[axis] + step, size)
            pl.semaphore_signal(
                barrier, inc=1, device_id={axis: peer}, device_id_type=pl.DeviceIdType.MESH
            )
            greeted += 1
    pl.semaphore_wait(barrier, greeted)

    def describe(item, step):
        kind, axis = plan[item]
        size = sizes[axis]
        peer = lax.rem(me[axis] + step, size)
        if kind == "gather":
            rows = ins[item].shape[0]
            source = ins[item]
            target = outs[item].at[pl.ds(pl.multiple_of(me[axis] * rows, rows), rows)]
        elif kind == "scatter":
            rows = outs[item].shape[0]
            source = ins[item].at[pl.ds(pl.multiple_of(peer * rows, rows), rows)]
            target = slots[item].at[me[axis]]
        else:
            source, target = ins[item], slots[item].at[me[axis]]
        return pltpu.make_async_remote_copy(
            src_ref=source,
            dst_ref=target,
            send_sem=send_sem.at[item, step],
            recv_sem=recv_sem.at[item, step],
            device_id={axis: peer},
            device_id_type=pl.DeviceIdType.MESH,
        )

    def arrival(item, step):
        kind, axis = plan[item]
        size = sizes[axis]
        origin = lax.rem(me[axis] + size - step, size)
        if kind == "gather":
            rows = ins[item].shape[0]
            target = outs[item].at[pl.ds(pl.multiple_of(origin * rows, rows), rows)]
        else:
            target = slots[item].at[origin]
        return pltpu.make_async_remote_copy(
            src_ref=target,
            dst_ref=target,
            send_sem=send_sem.at[item, step],
            recv_sem=recv_sem.at[item, step],
            device_id={axis: origin},
            device_id_type=pl.DeviceIdType.MESH,
        )

    most = max(sizes[axis] for axis in axes)
    sent = []
    for step in range(1, most):
        for item in range(count):
            if step < sizes[plan[item][1]]:
                copy = describe(item, step)
                copy.start()
                sent.append(copy)
    for item in range(count):
        kind, axis = plan[item]
        if kind == "gather":
            rows = ins[item].shape[0]
            outs[item][pl.ds(pl.multiple_of(me[axis] * rows, rows), rows), :] = ins[item][...]
        elif kind == "sum":
            slots[item][me[axis]] = ins[item][...]
    for item in range(count):
        kind, axis = plan[item]
        size = sizes[axis]
        for step in range(1, size):
            arrival(item, step).wait_recv()
        if kind == "scatter":
            rows = outs[item].shape[0]
            total = ins[item][pl.ds(pl.multiple_of(me[axis] * rows, rows), rows), :].astype(jnp.float32)
            for step in range(1, size):
                origin = lax.rem(me[axis] + size - step, size)
                total = total + slots[item][origin].astype(jnp.float32)
            outs[item][...] = total
        elif kind == "sum":
            total = slots[item][0].astype(jnp.float32)
            for index in range(1, size):
                total = total + slots[item][index].astype(jnp.float32)
            outs[item][...] = total
    for copy in sent:
        copy.wait_send()


def exchange(identity, *items):
    sizes = {axis: lax.axis_size(axis) for _, axis, _ in items}
    plan, shapes, slots = [], [], []
    for kind, axis, array in items:
        size = sizes[axis]
        rows, columns = array.shape
        plan.append((kind, axis))
        if kind == "gather":
            shapes.append(jax.ShapeDtypeStruct((size * rows, columns), array.dtype))
            slots.append(pltpu.VMEM((1, 16, 128), array.dtype))
        elif kind == "scatter":
            shapes.append(jax.ShapeDtypeStruct((rows // size, columns), jnp.float32))
            slots.append(pltpu.VMEM((size, rows // size, columns), array.dtype))
        else:
            shapes.append(jax.ShapeDtypeStruct((rows, columns), jnp.float32))
            slots.append(pltpu.VMEM((size, rows, columns), array.dtype))
    most = max(sizes.values())
    return pl.pallas_call(
        partial(exchange_kernel, tuple(plan), sizes),
        out_shape=tuple(shapes),
        in_specs=[pl.BlockSpec(memory_space=pltpu.VMEM)] * len(items),
        out_specs=tuple([pl.BlockSpec(memory_space=pltpu.VMEM)] * len(items)),
        scratch_shapes=slots
        + [
            pltpu.SemaphoreType.DMA((len(items), most)),
            pltpu.SemaphoreType.DMA((len(items), most)),
        ],
        compiler_params=pltpu.CompilerParams(
            collective_id=identity, has_side_effects=True, vmem_limit_bytes=48 * 2**20
        ),
    )(*[array for _, _, array in items])


def contract_rows(left_side, right_side):
    return lax.dot_general(
        left_side, right_side, (((0,), (0,)), ((), ())), preferred_element_type=jnp.float32
    )


def times_transposed(left_side, right_side):
    return lax.dot_general(
        left_side, right_side, (((1,), (1,)), ((), ())), preferred_element_type=jnp.float32
    )


def project(normed, weight):
    return jnp.dot(normed, weight, preferred_element_type=jnp.float32)


def on_device(
    layer_input,
    lengths,
    input_gain,
    proj_gate,
    proj_values,
    proj_state,
    proj_step,
    conv_values,
    bias_values,
    conv_state,
    bias_state,
    step_bias,
    decay_log,
    skip_gain,
    mixer_gain,
    proj_output,
    out_grad,
):
    local_rows = layer_input.shape[0]
    rows_in = layer_input.astype(jnp.float32)
    inv_rms = lax.rsqrt(jnp.mean(rows_in * rows_in, axis=1, keepdims=True) + epsilon)
    normed_rows = (rows_in * inv_rms * input_gain).astype(jnp.bfloat16)
    state_columns = proj_state.shape[1]
    head_count = proj_step.shape[1]
    tail = -(state_columns + head_count) % 128
    small_w = jnp.concatenate(
        [proj_state, proj_step, jnp.zeros((proj_step.shape[0], tail), jnp.bfloat16)], axis=1
    )
    normed, gate_w, values_w, small_w = exchange(
        0,
        ("gather", "tensor", normed_rows),
        ("gather", "dp", proj_gate),
        ("gather", "dp", proj_values),
        ("gather", "dp", small_w),
    )
    state_w = small_w[:, :state_columns]
    step_w = small_w[:, state_columns : state_columns + head_count]
    output_w = lax.all_gather(proj_output, "dp", axis=0, tiled=True)
    upstream = lax.all_gather(out_grad, "tensor", axis=0, tiled=True)
    gate_in = project(normed, gate_w)
    values_in = project(normed, values_w)
    state_in = project(normed, state_w)
    step_in = project(normed, step_w)
    present = (jnp.arange(normed.shape[0]) < lengths[0]).astype(jnp.float32)
    core = partial(mixer_core, present=present)
    gated, core_pull = jax.vjp(
        core,
        gate_in,
        values_in,
        state_in,
        step_in,
        conv_values,
        bias_values,
        conv_state,
        bias_state,
        step_bias,
        decay_log,
        skip_gain,
    )
    grad_normed_out = jnp.dot(upstream, output_w, preferred_element_type=jnp.float32)
    scaled_grad = grad_normed_out * mixer_gain
    row_sums = jnp.stack([jnp.sum(gated * gated, axis=1), jnp.sum(scaled_grad * gated, axis=1)])
    (row_sums,) = exchange(
        1, ("sum", "tensor", jnp.pad(row_sums, ((0, 6), (0, 0))))
    )
    inv_norm = lax.rsqrt(row_sums[0] / INNER + epsilon)[:, None]
    cross = row_sums[1]
    normed_out = (gated * inv_norm * mixer_gain).astype(jnp.bfloat16)
    mixed_rows = lax.psum_scatter(
        times_transposed(normed_out, output_w), "tensor", scatter_dimension=0, tiled=True
    )
    layer_output = (rows_in + mixed_rows).astype(jnp.bfloat16)
    grad_output_w = contract_rows(upstream, normed_out)
    grad_mixer_gain = jnp.sum(grad_normed_out * gated * inv_norm, axis=0)
    grad_gated = (
        inv_norm * scaled_grad - gated * (inv_norm * inv_norm * inv_norm) * (cross / INNER)[:, None]
    )
    (
        grad_gate_in,
        grad_values_in,
        grad_state_part,
        grad_step_in,
        grad_conv_values,
        grad_bias_values,
        grad_conv_part,
        grad_shift_part,
        grad_step_bias,
        grad_decay_log,
        grad_skip_gain,
    ) = core_pull(grad_gated)
    (own_state,) = exchange(2, ("scatter", "tensor", grad_state_part.astype(jnp.bfloat16)))
    own_state = own_state.astype(jnp.bfloat16)
    low_gate = grad_gate_in.astype(jnp.bfloat16)
    low_values = grad_values_in.astype(jnp.bfloat16)
    low_step = grad_step_in.astype(jnp.bfloat16)
    grad_gate_w = contract_rows(normed, low_gate)
    grad_values_w = contract_rows(normed, low_values)
    grad_small_w = jnp.concatenate(
        [
            contract_rows(normed_rows, own_state),
            contract_rows(normed, low_step),
            jnp.zeros((normed.shape[1], tail), jnp.float32),
        ],
        axis=1,
    )
    summed = times_transposed(low_gate, gate_w)
    summed = summed + times_transposed(low_values, values_w)
    head_part = summed + times_transposed(low_step, step_w)
    head_part, owned_gate, owned_values, owned_output, owned_small = exchange(
        3,
        ("scatter", "tensor", head_part.astype(jnp.bfloat16)),
        ("scatter", "dp", grad_gate_w.astype(jnp.bfloat16)),
        ("scatter", "dp", grad_values_w.astype(jnp.bfloat16)),
        ("scatter", "dp", grad_output_w.astype(jnp.bfloat16)),
        ("scatter", "dp", grad_small_w.astype(jnp.bfloat16)),
    )
    grad_normed_rows = head_part + times_transposed(own_state, state_w)
    scaled_in = grad_normed_rows * input_gain
    cross_in = jnp.mean(scaled_in * rows_in, axis=1, keepdims=True)
    input_grad = (
        out_grad.astype(jnp.float32)
        + inv_rms * scaled_in
        - rows_in * (inv_rms * inv_rms * inv_rms) * cross_in
    ).astype(jnp.bfloat16)
    grad_gain_part = jnp.sum(grad_normed_rows * rows_in * inv_rms, axis=0)
    width = grad_gain_part.shape[0]
    channels = grad_bias_values.shape[0]

    def packed(parts, columns):
        flat = jnp.concatenate([part.reshape(-1) for part in parts])
        filled = -(-flat.shape[0] // (8 * columns)) * 8 * columns
        return jnp.pad(flat, (0, filled - flat.shape[0])).reshape(-1, columns)

    def unpacked(table, parts):
        flat, start, out = table.reshape(-1), 0, []
        for part in parts:
            out.append(flat[start : start + part.size].reshape(part.shape))
            start += part.size
        return out

    shared = [grad_gain_part, grad_conv_part, grad_shift_part]
    shared_sum, owned_state = exchange(
        4,
        ("sum", "tensor", packed(shared, width)),
        ("sum", "tensor", owned_small[:, :state_columns]),
    )
    own = [
        grad_conv_values,
        grad_bias_values,
        grad_mixer_gain,
        grad_step_bias,
        grad_decay_log,
        grad_skip_gain,
    ]
    shared_sum, own_sum = exchange(
        5,
        ("sum", "dp", shared_sum),
        ("sum", "dp", packed(own, channels)),
    )
    grad_gain, grad_conv_state, grad_bias_state = unpacked(shared_sum, shared)
    (
        grad_conv_values,
        grad_bias_values,
        grad_mixer_gain,
        grad_step_bias,
        grad_decay_log,
        grad_skip_gain,
    ) = unpacked(own_sum, own)
    return (
        layer_output,
        input_grad,
        grad_gain,
        owned_gate,
        owned_values,
        owned_state,
        owned_small[:, state_columns : state_columns + head_count],
        grad_conv_values,
        grad_bias_values,
        grad_conv_state,
        grad_bias_state,
        grad_step_bias,
        grad_decay_log,
        grad_skip_gain,
        grad_mixer_gain,
        owned_output,
    )


def solution(mesh):
    return jax.shard_map(
        on_device,
        mesh=mesh,
        in_specs=(
            P(("dp", "tensor"), None),
            P("dp"),
            P(),
            P("dp", "tensor"),
            P("dp", "tensor"),
            P("dp", None),
            P("dp", "tensor"),
            P(None, "tensor"),
            P("tensor"),
            P(),
            P(),
            P("tensor"),
            P("tensor"),
            P("tensor"),
            P("tensor"),
            P("dp", "tensor"),
            P(("dp", "tensor"), None),
        ),
        out_specs=(
            P(("dp", "tensor"), None),
            P(("dp", "tensor"), None),
            P(),
            P("dp", "tensor"),
            P("dp", "tensor"),
            P("dp", None),
            P("dp", "tensor"),
            P(None, "tensor"),
            P("tensor"),
            P(),
            P(),
            P("tensor"),
            P("tensor"),
            P("tensor"),
            P("tensor"),
            P("dp", "tensor"),
        ),
        check_vma=False,
    )
```

```python
from functools import partial

import jax
import jax.numpy as jnp
from jax import lax
from jax.experimental import pallas as pl
from jax.experimental.pallas import tpu as pltpu
from jax.sharding import PartitionSpec as P

CONV = 4
BLOCK = 256
INNER = 2048


HIGHEST = lax.Precision.HIGHEST
epsilon = 1e-05


def rounded(v):
    return v + lax.stop_gradient(v.astype(jnp.bfloat16).astype(jnp.float32) - v)


def causal_conv(values, kernel, conv_shift):
    length = values.shape[0]
    padded = jnp.pad(values, ((CONV - 1, 0), (0, 0)))
    summed = conv_shift + jnp.zeros_like(values)
    for offset in range(CONV):
        summed = summed + kernel[offset] * padded[offset : offset + length]
    return summed


def rows_by_rows(left_side, right_side):
    return lax.dot_general(
        left_side, right_side, (((0,), (0,)), ((), ())), preferred_element_type=jnp.float32
    )


def columns_by_columns(left_side, right_side):
    return lax.dot_general(
        left_side, right_side, (((1,), (1,)), ((), ())), preferred_element_type=jnp.float32
    )


def causal_mask(length):
    return lax.broadcasted_iota(jnp.int32, (length, length), 0) >= lax.broadcasted_iota(
        jnp.int32, (length, length), 1
    )


def forward_kernel(values_ref, maps_ref, step_ref, cum_ref, across_ref, out_ref, kept_ref, state):
    heads = step_ref.shape[1]
    length, channels = values_ref.shape
    dim = channels // heads
    width = maps_ref.shape[1] // 2

    @pl.when(pl.program_id(0) == 0)
    def _():
        state[...] = jnp.zeros_like(state)

    kept_ref[0] = state[...]
    input_map, output_map = maps_ref[:, :width], maps_ref[:, width:]
    scores = columns_by_columns(output_map, input_map)
    carried = columns_by_columns(output_map, state[...].astype(jnp.bfloat16))
    mask = causal_mask(length)
    remains = []
    for head in range(heads):
        part = slice(head * dim, (head + 1) * dim)
        cum = cum_ref[:, head : head + 1]
        across = across_ref[head : head + 1, :]
        decays = jnp.exp(jnp.where(mask, cum - across, -10000.0))
        weights = (scores * decays).astype(jnp.bfloat16)
        scaled = (values_ref[:, part].astype(jnp.float32) * step_ref[:, head : head + 1]).astype(
            jnp.bfloat16
        )
        inside = jnp.dot(weights, scaled, preferred_element_type=jnp.float32)
        out_ref[:, part] = inside + carried[:, part] * jnp.exp(cum)
        last = across[:, length - 1 : length]
        remains.append((scaled.astype(jnp.float32) * jnp.exp(last - cum)).astype(jnp.bfloat16))
        state[part, :] = state[part, :] * jnp.exp(last)
    state[...] += rows_by_rows(jnp.concatenate(remains, axis=1), input_map)


def backward_kernel(
    values_ref, maps_ref, step_ref, cum_ref, across_ref, kept_ref, grad_ref,
    grad_values_ref, grad_maps_ref, grad_step_ref, grad_cum_ref, grad_across_ref, grad_state,
):
    heads = step_ref.shape[1]
    length, channels = values_ref.shape
    dim = channels // heads
    width = maps_ref.shape[1] // 2

    @pl.when(pl.program_id(0) == 0)
    def _():
        grad_state[...] = jnp.zeros_like(grad_state)

    input_map, output_map = maps_ref[:, :width], maps_ref[:, width:]
    scores = columns_by_columns(output_map, input_map)
    kept = kept_ref[0].astype(jnp.bfloat16)
    low_state = grad_state[...].astype(jnp.bfloat16)
    carried = columns_by_columns(output_map, kept)
    pulled = columns_by_columns(input_map, low_state)
    mask = causal_mask(length)
    is_last = lax.broadcasted_iota(jnp.int32, (1, length), 1) == length - 1
    grad_scores = jnp.zeros((length, length), jnp.float32)
    faded, remains = [], []
    for head in range(heads):
        part = slice(head * dim, (head + 1) * dim)
        cum = cum_ref[:, head : head + 1]
        across = across_ref[head : head + 1, :]
        step = step_ref[:, head : head + 1]
        values = values_ref[:, part].astype(jnp.float32)
        decays = jnp.exp(jnp.where(mask, cum - across, -10000.0))
        spread = scores * decays
        weights = spread.astype(jnp.bfloat16)
        scaled = (values * step).astype(jnp.bfloat16)
        grad = grad_ref[:, part]
        low_grad = grad.astype(jnp.bfloat16)
        grad_weights = columns_by_columns(low_grad, scaled)
        grad_scores += grad_weights * decays
        product = grad_weights * spread
        last = across[:, length - 1 : length]
        remain = jnp.exp(last - cum)
        kept_scaled = scaled.astype(jnp.float32) * remain
        grad_remain = jnp.sum(kept_scaled * pulled[:, part], axis=1, keepdims=True)
        faded_grad = grad * jnp.exp(cum)
        grad_cum_ref[:, head : head + 1] = (
            jnp.sum(product, axis=1, keepdims=True)
            + jnp.sum(faded_grad * carried[:, part], axis=1, keepdims=True)
            - grad_remain
        )
        on_last = jnp.sum(grad_remain, axis=0, keepdims=True) + jnp.exp(last) * jnp.sum(
            jnp.sum(kept_ref[0, part, :] * grad_state[part, :], axis=1, keepdims=True),
            axis=0,
            keepdims=True,
        )
        grad_across_ref[head : head + 1, :] = (
            jnp.where(is_last, on_last, 0.0) - jnp.sum(product, axis=0, keepdims=True)
        )
        grad_scaled = rows_by_rows(weights, low_grad) + remain * pulled[:, part]
        grad_values_ref[:, part] = grad_scaled * step
        grad_step_ref[:, head : head + 1] = jnp.sum(grad_scaled * values, axis=1, keepdims=True)
        faded.append(faded_grad.astype(jnp.bfloat16))
        remains.append(kept_scaled.astype(jnp.bfloat16))
        grad_state[part, :] = grad_state[part, :] * jnp.exp(last)
    all_faded = jnp.concatenate(faded, axis=1)
    all_remains = jnp.concatenate(remains, axis=1)
    low_scores = grad_scores.astype(jnp.bfloat16)
    grad_maps_ref[:, :width] = rows_by_rows(low_scores, output_map) + jnp.dot(
        all_remains, low_state, preferred_element_type=jnp.float32
    )
    grad_maps_ref[:, width:] = jnp.dot(
        low_scores, input_map, preferred_element_type=jnp.float32
    ) + jnp.dot(all_faded, kept, preferred_element_type=jnp.float32)
    grad_state[...] += rows_by_rows(all_faded, output_map)


def scan_specs(length, channels, maps, heads, place):
    return [
        pl.BlockSpec((BLOCK, channels), lambda i: (place(i), 0)),
        pl.BlockSpec((BLOCK, maps), lambda i: (place(i), 0)),
        pl.BlockSpec((BLOCK, heads), lambda i: (place(i), 0)),
        pl.BlockSpec((BLOCK, heads), lambda i: (place(i), 0)),
        pl.BlockSpec((heads, BLOCK), lambda i: (0, place(i))),
    ]


def scan_forward(values, maps, step_sizes, cum):
    length, channels = values.shape
    heads, columns = step_sizes.shape[1], maps.shape[1]
    blocks = length // BLOCK
    return pl.pallas_call(
        forward_kernel,
        grid=(blocks,),
        out_shape=(
            jax.ShapeDtypeStruct((length, channels), jnp.float32),
            jax.ShapeDtypeStruct((blocks, channels, columns // 2), jnp.float32),
        ),
        in_specs=scan_specs(length, channels, columns, heads, lambda i: i),
        out_specs=(
            pl.BlockSpec((BLOCK, channels), lambda i: (i, 0)),
            pl.BlockSpec((1, channels, columns // 2), lambda i: (i, 0, 0)),
        ),
        scratch_shapes=[pltpu.VMEM((channels, columns // 2), jnp.float32)],
        compiler_params=pltpu.CompilerParams(vmem_limit_bytes=24 * 2**20),
    )(values, maps, step_sizes, cum, cum.T)


def scan_backward(values, maps, step_sizes, cum, kept, grad):
    length, channels = values.shape
    heads, columns = step_sizes.shape[1], maps.shape[1]
    blocks = length // BLOCK

    def place(i):
        return blocks - 1 - i

    specs = scan_specs(length, channels, columns, heads, place)
    grad_values, grad_maps, grad_step, grad_cum, grad_across = pl.pallas_call(
        backward_kernel,
        grid=(blocks,),
        out_shape=(
            jax.ShapeDtypeStruct((length, channels), jnp.float32),
            jax.ShapeDtypeStruct((length, columns), jnp.float32),
            jax.ShapeDtypeStruct((length, heads), jnp.float32),
            jax.ShapeDtypeStruct((length, heads), jnp.float32),
            jax.ShapeDtypeStruct((heads, length), jnp.float32),
        ),
        in_specs=specs
        + [
            pl.BlockSpec((1, channels, columns // 2), lambda i: (place(i), 0, 0)),
            pl.BlockSpec((BLOCK, channels), lambda i: (place(i), 0)),
        ],
        out_specs=tuple(specs),
        scratch_shapes=[pltpu.VMEM((channels, columns // 2), jnp.float32)],
        compiler_params=pltpu.CompilerParams(vmem_limit_bytes=24 * 2**20),
    )(values, maps, step_sizes, cum, cum.T, kept, grad)
    return grad_values, grad_maps, grad_step, grad_cum + grad_across.T


def before_scan(
    values_in,
    state_in,
    step_in,
    conv_values,
    bias_values,
    conv_state,
    bias_state,
    step_bias,
    decay_log,
    present,
):
    values = rounded(jax.nn.silu(causal_conv(values_in, conv_values, bias_values)))
    maps = rounded(jax.nn.silu(causal_conv(state_in, conv_state, bias_state)))
    step_sizes = jax.nn.softplus(step_in + step_bias) * present[:, None]
    length, heads = step_sizes.shape
    changes = (step_sizes * -jnp.exp(decay_log)).reshape(length // BLOCK, BLOCK, heads)
    lower = causal_mask(BLOCK).astype(jnp.float32)
    cum = jnp.einsum("ij,bjh->bih", lower, changes, precision=HIGHEST)
    return values, maps, step_sizes, cum.reshape(length, heads)


def after_scan(scanned, values, gate_in, skip_gain, present):
    skip = jnp.repeat(skip_gain, values.shape[1] // skip_gain.shape[0])
    return (scanned + skip * values) * present[:, None] * jax.nn.silu(gate_in)


def exchange_kernel(plan, sizes, *refs):
    count = len(plan)
    ins, outs = refs[:count], refs[count : 2 * count]
    slots = refs[2 * count : 3 * count]
    send_sem, recv_sem = refs[3 * count :]
    axes = sorted({axis for _, axis in plan})
    me = {axis: lax.axis_index(axis) for axis in axes}
    barrier = pltpu.get_barrier_semaphore()
    greeted = 0
    for axis in axes:
        size = sizes[axis]
        for step in range(1, size):
            peer = lax.rem(me[axis] + step, size)
            pl.semaphore_signal(
                barrier, inc=1, device_id={axis: peer}, device_id_type=pl.DeviceIdType.MESH
            )
            greeted += 1
    pl.semaphore_wait(barrier, greeted)

    def describe(item, step):
        kind, axis = plan[item]
        size = sizes[axis]
        peer = lax.rem(me[axis] + step, size)
        if kind == "gather":
            rows = ins[item].shape[0]
            source = ins[item]
            target = outs[item].at[pl.ds(pl.multiple_of(me[axis] * rows, rows), rows)]
        elif kind == "scatter":
            rows = outs[item].shape[0]
            source = ins[item].at[pl.ds(pl.multiple_of(peer * rows, rows), rows)]
            target = slots[item].at[me[axis]]
        else:
            source, target = ins[item], slots[item].at[me[axis]]
        return pltpu.make_async_remote_copy(
            src_ref=source,
            dst_ref=target,
            send_sem=send_sem.at[item, step],
            recv_sem=recv_sem.at[item, step],
            device_id={axis: peer},
            device_id_type=pl.DeviceIdType.MESH,
        )

    def arrival(item, step):
        kind, axis = plan[item]
        size = sizes[axis]
        origin = lax.rem(me[axis] + size - step, size)
        if kind == "gather":
            rows = ins[item].shape[0]
            target = outs[item].at[pl.ds(pl.multiple_of(origin * rows, rows), rows)]
        else:
            target = slots[item].at[origin]
        return pltpu.make_async_remote_copy(
            src_ref=target,
            dst_ref=target,
            send_sem=send_sem.at[item, step],
            recv_sem=recv_sem.at[item, step],
            device_id={axis: origin},
            device_id_type=pl.DeviceIdType.MESH,
        )

    most = max(sizes[axis] for axis in axes)
    sent = []
    for step in range(1, most):
        for item in range(count):
            if step < sizes[plan[item][1]]:
                copy = describe(item, step)
                copy.start()
                sent.append(copy)
    for item in range(count):
        kind, axis = plan[item]
        if kind == "gather":
            rows = ins[item].shape[0]
            outs[item][pl.ds(pl.multiple_of(me[axis] * rows, rows), rows), :] = ins[item][...]
        elif kind == "sum":
            slots[item][me[axis]] = ins[item][...]
    for item in range(count):
        kind, axis = plan[item]
        size = sizes[axis]
        for step in range(1, size):
            arrival(item, step).wait_recv()
        if kind == "scatter":
            rows = outs[item].shape[0]
            total = ins[item][pl.ds(pl.multiple_of(me[axis] * rows, rows), rows), :].astype(jnp.float32)
            for step in range(1, size):
                origin = lax.rem(me[axis] + size - step, size)
                total = total + slots[item][origin].astype(jnp.float32)
            outs[item][...] = total
        elif kind == "sum":
            total = slots[item][0].astype(jnp.float32)
            for index in range(1, size):
                total = total + slots[item][index].astype(jnp.float32)
            outs[item][...] = total
    for copy in sent:
        copy.wait_send()


def exchange(identity, *items):
    sizes = {axis: lax.axis_size(axis) for _, axis, _ in items}
    plan, shapes, slots = [], [], []
    for kind, axis, array in items:
        size = sizes[axis]
        rows, columns = array.shape
        plan.append((kind, axis))
        if kind == "gather":
            shapes.append(jax.ShapeDtypeStruct((size * rows, columns), array.dtype))
            slots.append(pltpu.VMEM((1, 16, 128), array.dtype))
        elif kind == "scatter":
            shapes.append(jax.ShapeDtypeStruct((rows // size, columns), jnp.float32))
            slots.append(pltpu.VMEM((size, rows // size, columns), array.dtype))
        else:
            shapes.append(jax.ShapeDtypeStruct((rows, columns), jnp.float32))
            slots.append(pltpu.VMEM((size, rows, columns), array.dtype))
    most = max(sizes.values())
    return pl.pallas_call(
        partial(exchange_kernel, tuple(plan), sizes),
        out_shape=tuple(shapes),
        in_specs=[pl.BlockSpec(memory_space=pltpu.VMEM)] * len(items),
        out_specs=tuple([pl.BlockSpec(memory_space=pltpu.VMEM)] * len(items)),
        scratch_shapes=slots
        + [
            pltpu.SemaphoreType.DMA((len(items), most)),
            pltpu.SemaphoreType.DMA((len(items), most)),
        ],
        compiler_params=pltpu.CompilerParams(
            collective_id=identity, has_side_effects=True, vmem_limit_bytes=24 * 2**20
        ),
    )(*[array for _, _, array in items])


def contract_rows(left_side, right_side):
    return lax.dot_general(
        left_side, right_side, (((0,), (0,)), ((), ())), preferred_element_type=jnp.float32
    )


def times_transposed(left_side, right_side):
    return lax.dot_general(
        left_side, right_side, (((1,), (1,)), ((), ())), preferred_element_type=jnp.float32
    )


def project(normed, weight):
    return jnp.dot(normed, weight, preferred_element_type=jnp.float32)


def on_device(
    layer_input,
    lengths,
    input_gain,
    proj_gate,
    proj_values,
    proj_state,
    proj_step,
    conv_values,
    bias_values,
    conv_state,
    bias_state,
    step_bias,
    decay_log,
    skip_gain,
    mixer_gain,
    proj_output,
    out_grad,
):
    local_rows = layer_input.shape[0]
    rows_in = layer_input.astype(jnp.float32)
    inv_rms = lax.rsqrt(jnp.mean(rows_in * rows_in, axis=1, keepdims=True) + epsilon)
    normed_rows = (rows_in * inv_rms * input_gain).astype(jnp.bfloat16)
    state_columns = proj_state.shape[1]
    head_count = proj_step.shape[1]
    tail = -(state_columns + head_count) % 128
    small_w = jnp.concatenate(
        [proj_state, proj_step, jnp.zeros((proj_step.shape[0], tail), jnp.bfloat16)], axis=1
    )
    normed, gate_w, values_w, small_w = exchange(
        0,
        ("gather", "tensor", normed_rows),
        ("gather", "dp", proj_gate),
        ("gather", "dp", proj_values),
        ("gather", "dp", small_w),
    )
    state_w = small_w[:, :state_columns]
    step_w = small_w[:, state_columns : state_columns + head_count]
    output_w = lax.all_gather(proj_output, "dp", axis=0, tiled=True)
    upstream = lax.all_gather(out_grad, "tensor", axis=0, tiled=True)
    gate_in = project(normed, gate_w)
    values_in = project(normed, values_w)
    state_in = project(normed, state_w)
    step_in = project(normed, step_w)
    present = (jnp.arange(normed.shape[0]) < lengths[0]).astype(jnp.float32)
    (values, maps, step_sizes, cum), before_pull = jax.vjp(
        partial(before_scan, present=present),
        values_in,
        state_in,
        step_in,
        conv_values,
        bias_values,
        conv_state,
        bias_state,
        step_bias,
        decay_log,
    )
    low_values, low_maps = values.astype(jnp.bfloat16), maps.astype(jnp.bfloat16)
    scanned, kept = scan_forward(low_values, low_maps, step_sizes, cum)
    gated, after_pull = jax.vjp(
        partial(after_scan, present=present), scanned, values, gate_in, skip_gain
    )
    grad_normed_out = jnp.dot(upstream, output_w, preferred_element_type=jnp.float32)
    scaled_grad = grad_normed_out * mixer_gain
    row_sums = jnp.stack([jnp.sum(gated * gated, axis=1), jnp.sum(scaled_grad * gated, axis=1)])
    (row_sums,) = exchange(
        1, ("sum", "tensor", jnp.pad(row_sums, ((0, 6), (0, 0))))
    )
    inv_norm = lax.rsqrt(row_sums[0] / INNER + epsilon)[:, None]
    cross = row_sums[1]
    normed_out = (gated * inv_norm * mixer_gain).astype(jnp.bfloat16)
    mixed_rows = lax.psum_scatter(
        times_transposed(normed_out, output_w), "tensor", scatter_dimension=0, tiled=True
    )
    layer_output = (rows_in + mixed_rows).astype(jnp.bfloat16)
    grad_output_w = contract_rows(upstream, normed_out)
    grad_mixer_gain = jnp.sum(grad_normed_out * gated * inv_norm, axis=0)
    grad_gated = (
        inv_norm * scaled_grad - gated * (inv_norm * inv_norm * inv_norm) * (cross / INNER)[:, None]
    )
    grad_scanned, grad_values, grad_gate_in, grad_skip_gain = after_pull(grad_gated)
    scan_values, grad_maps, grad_step, grad_cum = scan_backward(
        low_values, low_maps, step_sizes, cum, kept, grad_scanned
    )
    (
        grad_values_in,
        grad_state_part,
        grad_step_in,
        grad_conv_values,
        grad_bias_values,
        grad_conv_part,
        grad_shift_part,
        grad_step_bias,
        grad_decay_log,
    ) = before_pull((grad_values + scan_values, grad_maps, grad_step, grad_cum))
    (own_state,) = exchange(2, ("scatter", "tensor", grad_state_part.astype(jnp.bfloat16)))
    own_state = own_state.astype(jnp.bfloat16)
    low_gate = grad_gate_in.astype(jnp.bfloat16)
    low_values = grad_values_in.astype(jnp.bfloat16)
    low_step = grad_step_in.astype(jnp.bfloat16)
    grad_gate_w = contract_rows(normed, low_gate)
    grad_values_w = contract_rows(normed, low_values)
    grad_small_w = jnp.concatenate(
        [
            contract_rows(normed_rows, own_state),
            contract_rows(normed, low_step),
            jnp.zeros((normed.shape[1], tail), jnp.float32),
        ],
        axis=1,
    )
    summed = times_transposed(low_gate, gate_w)
    summed = summed + times_transposed(low_values, values_w)
    head_part = summed + times_transposed(low_step, step_w)
    head_part, owned_gate, owned_values, owned_output, owned_small = exchange(
        3,
        ("scatter", "tensor", head_part.astype(jnp.bfloat16)),
        ("scatter", "dp", grad_gate_w.astype(jnp.bfloat16)),
        ("scatter", "dp", grad_values_w.astype(jnp.bfloat16)),
        ("scatter", "dp", grad_output_w.astype(jnp.bfloat16)),
        ("scatter", "dp", grad_small_w.astype(jnp.bfloat16)),
    )
    grad_normed_rows = head_part + times_transposed(own_state, state_w)
    scaled_in = grad_normed_rows * input_gain
    cross_in = jnp.mean(scaled_in * rows_in, axis=1, keepdims=True)
    input_grad = (
        out_grad.astype(jnp.float32)
        + inv_rms * scaled_in
        - rows_in * (inv_rms * inv_rms * inv_rms) * cross_in
    ).astype(jnp.bfloat16)
    grad_gain_part = jnp.sum(grad_normed_rows * rows_in * inv_rms, axis=0)
    width = grad_gain_part.shape[0]
    channels = grad_bias_values.shape[0]

    def packed(parts, columns):
        flat = jnp.concatenate([part.reshape(-1) for part in parts])
        filled = -(-flat.shape[0] // (8 * columns)) * 8 * columns
        return jnp.pad(flat, (0, filled - flat.shape[0])).reshape(-1, columns)

    def unpacked(table, parts):
        flat, start, out = table.reshape(-1), 0, []
        for part in parts:
            out.append(flat[start : start + part.size].reshape(part.shape))
            start += part.size
        return out

    shared = [grad_gain_part, grad_conv_part, grad_shift_part]
    shared_sum, owned_state = exchange(
        4,
        ("sum", "tensor", packed(shared, width)),
        ("sum", "tensor", owned_small[:, :state_columns]),
    )
    own = [
        grad_conv_values,
        grad_bias_values,
        grad_mixer_gain,
        grad_step_bias,
        grad_decay_log,
        grad_skip_gain,
    ]
    shared_sum, own_sum = exchange(
        5,
        ("sum", "dp", shared_sum),
        ("sum", "dp", packed(own, channels)),
    )
    grad_gain, grad_conv_state, grad_bias_state = unpacked(shared_sum, shared)
    (
        grad_conv_values,
        grad_bias_values,
        grad_mixer_gain,
        grad_step_bias,
        grad_decay_log,
        grad_skip_gain,
    ) = unpacked(own_sum, own)
    return (
        layer_output,
        input_grad,
        grad_gain,
        owned_gate,
        owned_values,
        owned_state,
        owned_small[:, state_columns : state_columns + head_count],
        grad_conv_values,
        grad_bias_values,
        grad_conv_state,
        grad_bias_state,
        grad_step_bias,
        grad_decay_log,
        grad_skip_gain,
        grad_mixer_gain,
        owned_output,
    )


def solution(mesh):
    return jax.shard_map(
        on_device,
        mesh=mesh,
        in_specs=(
            P(("dp", "tensor"), None),
            P("dp"),
            P(),
            P("dp", "tensor"),
            P("dp", "tensor"),
            P("dp", None),
            P("dp", "tensor"),
            P(None, "tensor"),
            P("tensor"),
            P(),
            P(),
            P("tensor"),
            P("tensor"),
            P("tensor"),
            P("tensor"),
            P("dp", "tensor"),
            P(("dp", "tensor"), None),
        ),
        out_specs=(
            P(("dp", "tensor"), None),
            P(("dp", "tensor"), None),
            P(),
            P("dp", "tensor"),
            P("dp", "tensor"),
            P("dp", None),
            P("dp", "tensor"),
            P(None, "tensor"),
            P("tensor"),
            P(),
            P(),
            P("tensor"),
            P("tensor"),
            P("tensor"),
            P("tensor"),
            P("dp", "tensor"),
        ),
        check_vma=False,
    )
```

```python
from functools import partial

import jax
import jax.numpy as jnp
from jax import lax
from jax.experimental import pallas as pl
from jax.experimental.pallas import tpu as pltpu
from jax.sharding import PartitionSpec as P

CONV = 4
BLOCK = 256
INNER = 2048


HIGHEST = lax.Precision.HIGHEST
epsilon = 1e-05


def rounded(v):
    return v + lax.stop_gradient(v.astype(jnp.bfloat16).astype(jnp.float32) - v)


def causal_conv(values, kernel, conv_shift):
    length = values.shape[0]
    padded = jnp.pad(values, ((CONV - 1, 0), (0, 0)))
    summed = conv_shift + jnp.zeros_like(values)
    for offset in range(CONV):
        summed = summed + kernel[offset] * padded[offset : offset + length]
    return summed


def rows_by_rows(left_side, right_side):
    return lax.dot_general(
        left_side, right_side, (((0,), (0,)), ((), ())), preferred_element_type=jnp.float32
    )


def columns_by_columns(left_side, right_side):
    return lax.dot_general(
        left_side, right_side, (((1,), (1,)), ((), ())), preferred_element_type=jnp.float32
    )


def causal_mask(length):
    return lax.broadcasted_iota(jnp.int32, (length, length), 0) >= lax.broadcasted_iota(
        jnp.int32, (length, length), 1
    )


def forward_kernel(values_ref, maps_ref, step_ref, cum_ref, across_ref, out_ref, kept_ref, state):
    heads = step_ref.shape[1]
    length, channels = values_ref.shape
    dim = channels // heads
    width = maps_ref.shape[1] // 2

    @pl.when(pl.program_id(0) == 0)
    def _():
        state[...] = jnp.zeros_like(state)

    kept_ref[0] = state[...]
    input_map, output_map = maps_ref[:, :width], maps_ref[:, width:]
    scores = columns_by_columns(output_map, input_map)
    carried = columns_by_columns(output_map, state[...].astype(jnp.bfloat16))
    mask = causal_mask(length)
    remains = []
    for head in range(heads):
        part = slice(head * dim, (head + 1) * dim)
        cum = cum_ref[:, head : head + 1]
        across = across_ref[head : head + 1, :]
        decays = jnp.exp(jnp.where(mask, cum - across, -10000.0))
        weights = (scores * decays).astype(jnp.bfloat16)
        scaled = (values_ref[:, part].astype(jnp.float32) * step_ref[:, head : head + 1]).astype(
            jnp.bfloat16
        )
        inside = jnp.dot(weights, scaled, preferred_element_type=jnp.float32)
        out_ref[:, part] = inside + carried[:, part] * jnp.exp(cum)
        last = across[:, length - 1 : length]
        remains.append((scaled.astype(jnp.float32) * jnp.exp(last - cum)).astype(jnp.bfloat16))
        state[part, :] = state[part, :] * jnp.exp(last)
    state[...] += rows_by_rows(jnp.concatenate(remains, axis=1), input_map)


def backward_kernel(
    values_ref, maps_ref, step_ref, cum_ref, across_ref, kept_ref, grad_ref,
    grad_values_ref, grad_maps_ref, grad_step_ref, grad_cum_ref, grad_across_ref, grad_state,
):
    heads = step_ref.shape[1]
    length, channels = values_ref.shape
    dim = channels // heads
    width = maps_ref.shape[1] // 2

    @pl.when(pl.program_id(0) == 0)
    def _():
        grad_state[...] = jnp.zeros_like(grad_state)

    input_map, output_map = maps_ref[:, :width], maps_ref[:, width:]
    scores = columns_by_columns(output_map, input_map)
    kept = kept_ref[0].astype(jnp.bfloat16)
    low_state = grad_state[...].astype(jnp.bfloat16)
    carried = columns_by_columns(output_map, kept)
    pulled = columns_by_columns(input_map, low_state)
    mask = causal_mask(length)
    is_last = lax.broadcasted_iota(jnp.int32, (1, length), 1) == length - 1
    grad_scores = jnp.zeros((length, length), jnp.float32)
    faded, remains = [], []
    for head in range(heads):
        part = slice(head * dim, (head + 1) * dim)
        cum = cum_ref[:, head : head + 1]
        across = across_ref[head : head + 1, :]
        step = step_ref[:, head : head + 1]
        values = values_ref[:, part].astype(jnp.float32)
        decays = jnp.exp(jnp.where(mask, cum - across, -10000.0))
        spread = scores * decays
        weights = spread.astype(jnp.bfloat16)
        scaled = (values * step).astype(jnp.bfloat16)
        grad = grad_ref[:, part]
        low_grad = grad.astype(jnp.bfloat16)
        grad_weights = columns_by_columns(low_grad, scaled)
        grad_scores += grad_weights * decays
        product = grad_weights * spread
        last = across[:, length - 1 : length]
        remain = jnp.exp(last - cum)
        kept_scaled = scaled.astype(jnp.float32) * remain
        grad_remain = jnp.sum(kept_scaled * pulled[:, part], axis=1, keepdims=True)
        faded_grad = grad * jnp.exp(cum)
        grad_cum_ref[:, head : head + 1] = (
            jnp.sum(product, axis=1, keepdims=True)
            + jnp.sum(faded_grad * carried[:, part], axis=1, keepdims=True)
            - grad_remain
        )
        on_last = jnp.sum(grad_remain, axis=0, keepdims=True) + jnp.exp(last) * jnp.sum(
            jnp.sum(kept_ref[0, part, :] * grad_state[part, :], axis=1, keepdims=True),
            axis=0,
            keepdims=True,
        )
        grad_across_ref[head : head + 1, :] = (
            jnp.where(is_last, on_last, 0.0) - jnp.sum(product, axis=0, keepdims=True)
        )
        grad_scaled = rows_by_rows(weights, low_grad) + remain * pulled[:, part]
        grad_values_ref[:, part] = grad_scaled * step
        grad_step_ref[:, head : head + 1] = jnp.sum(grad_scaled * values, axis=1, keepdims=True)
        faded.append(faded_grad.astype(jnp.bfloat16))
        remains.append(kept_scaled.astype(jnp.bfloat16))
        grad_state[part, :] = grad_state[part, :] * jnp.exp(last)
    all_faded = jnp.concatenate(faded, axis=1)
    all_remains = jnp.concatenate(remains, axis=1)
    low_scores = grad_scores.astype(jnp.bfloat16)
    grad_maps_ref[:, :width] = rows_by_rows(low_scores, output_map) + jnp.dot(
        all_remains, low_state, preferred_element_type=jnp.float32
    )
    grad_maps_ref[:, width:] = jnp.dot(
        low_scores, input_map, preferred_element_type=jnp.float32
    ) + jnp.dot(all_faded, kept, preferred_element_type=jnp.float32)
    grad_state[...] += rows_by_rows(all_faded, output_map)


def scan_specs(length, channels, maps, heads, place):
    return [
        pl.BlockSpec((BLOCK, channels), lambda i: (place(i), 0)),
        pl.BlockSpec((BLOCK, maps), lambda i: (place(i), 0)),
        pl.BlockSpec((BLOCK, heads), lambda i: (place(i), 0)),
        pl.BlockSpec((BLOCK, heads), lambda i: (place(i), 0)),
        pl.BlockSpec((heads, BLOCK), lambda i: (0, place(i))),
    ]


def scan_forward(values, maps, step_sizes, cum):
    length, channels = values.shape
    heads, columns = step_sizes.shape[1], maps.shape[1]
    blocks = length // BLOCK
    return pl.pallas_call(
        forward_kernel,
        grid=(blocks,),
        out_shape=(
            jax.ShapeDtypeStruct((length, channels), jnp.float32),
            jax.ShapeDtypeStruct((blocks, channels, columns // 2), jnp.float32),
        ),
        in_specs=scan_specs(length, channels, columns, heads, lambda i: i),
        out_specs=(
            pl.BlockSpec((BLOCK, channels), lambda i: (i, 0)),
            pl.BlockSpec((1, channels, columns // 2), lambda i: (i, 0, 0)),
        ),
        scratch_shapes=[pltpu.VMEM((channels, columns // 2), jnp.float32)],
        compiler_params=pltpu.CompilerParams(vmem_limit_bytes=24 * 2**20),
    )(values, maps, step_sizes, cum, cum.T)


def scan_backward(values, maps, step_sizes, cum, kept, grad):
    length, channels = values.shape
    heads, columns = step_sizes.shape[1], maps.shape[1]
    blocks = length // BLOCK

    def place(i):
        return blocks - 1 - i

    specs = scan_specs(length, channels, columns, heads, place)
    grad_values, grad_maps, grad_step, grad_cum, grad_across = pl.pallas_call(
        backward_kernel,
        grid=(blocks,),
        out_shape=(
            jax.ShapeDtypeStruct((length, channels), jnp.float32),
            jax.ShapeDtypeStruct((length, columns), jnp.float32),
            jax.ShapeDtypeStruct((length, heads), jnp.float32),
            jax.ShapeDtypeStruct((length, heads), jnp.float32),
            jax.ShapeDtypeStruct((heads, length), jnp.float32),
        ),
        in_specs=specs
        + [
            pl.BlockSpec((1, channels, columns // 2), lambda i: (place(i), 0, 0)),
            pl.BlockSpec((BLOCK, channels), lambda i: (place(i), 0)),
        ],
        out_specs=tuple(specs),
        scratch_shapes=[pltpu.VMEM((channels, columns // 2), jnp.float32)],
        compiler_params=pltpu.CompilerParams(vmem_limit_bytes=24 * 2**20),
    )(values, maps, step_sizes, cum, cum.T, kept, grad)
    return grad_values, grad_maps, grad_step, grad_cum + grad_across.T


def before_scan(
    values_in,
    state_in,
    step_in,
    conv_values,
    bias_values,
    conv_state,
    bias_state,
    step_bias,
    decay_log,
    present,
):
    values = rounded(jax.nn.silu(causal_conv(values_in, conv_values, bias_values)))
    maps = rounded(jax.nn.silu(causal_conv(state_in, conv_state, bias_state)))
    step_sizes = jax.nn.softplus(step_in + step_bias) * present[:, None]
    length, heads = step_sizes.shape
    changes = (step_sizes * -jnp.exp(decay_log)).reshape(length // BLOCK, BLOCK, heads)
    lower = causal_mask(BLOCK).astype(jnp.float32)
    cum = jnp.einsum("ij,bjh->bih", lower, changes, precision=HIGHEST)
    return values, maps, step_sizes, cum.reshape(length, heads)


def after_scan(scanned, values, gate_in, skip_gain, present):
    skip = jnp.repeat(skip_gain, values.shape[1] // skip_gain.shape[0])
    return (scanned + skip * values) * present[:, None] * jax.nn.silu(gate_in)


def exchange_kernel(plan, sizes, *refs):
    count = len(plan)
    ins, outs = refs[:count], refs[count : 2 * count]
    slots = refs[2 * count : 3 * count]
    send_sem, recv_sem = refs[3 * count :]
    axes = sorted({axis for _, axis in plan})
    me = {axis: lax.axis_index(axis) for axis in axes}
    barrier = pltpu.get_barrier_semaphore()
    greeted = 0
    for axis in axes:
        size = sizes[axis]
        for step in range(1, size):
            peer = lax.rem(me[axis] + step, size)
            pl.semaphore_signal(
                barrier, inc=1, device_id={axis: peer}, device_id_type=pl.DeviceIdType.MESH
            )
            greeted += 1
    pl.semaphore_wait(barrier, greeted)

    def describe(item, step):
        kind, axis = plan[item]
        size = sizes[axis]
        peer = lax.rem(me[axis] + step, size)
        if kind == "gather":
            rows = ins[item].shape[0]
            source = ins[item]
            target = outs[item].at[pl.ds(pl.multiple_of(me[axis] * rows, rows), rows)]
        elif kind == "scatter":
            rows = outs[item].shape[0]
            source = ins[item].at[pl.ds(pl.multiple_of(peer * rows, rows), rows)]
            target = slots[item].at[me[axis]]
        else:
            source, target = ins[item], slots[item].at[me[axis]]
        return pltpu.make_async_remote_copy(
            src_ref=source,
            dst_ref=target,
            send_sem=send_sem.at[item, step],
            recv_sem=recv_sem.at[item, step],
            device_id={axis: peer},
            device_id_type=pl.DeviceIdType.MESH,
        )

    def arrival(item, step):
        kind, axis = plan[item]
        size = sizes[axis]
        origin = lax.rem(me[axis] + size - step, size)
        if kind == "gather":
            rows = ins[item].shape[0]
            target = outs[item].at[pl.ds(pl.multiple_of(origin * rows, rows), rows)]
        else:
            target = slots[item].at[origin]
        return pltpu.make_async_remote_copy(
            src_ref=target,
            dst_ref=target,
            send_sem=send_sem.at[item, step],
            recv_sem=recv_sem.at[item, step],
            device_id={axis: origin},
            device_id_type=pl.DeviceIdType.MESH,
        )

    most = max(sizes[axis] for axis in axes)
    sent = []
    for step in range(1, most):
        for item in range(count):
            if step < sizes[plan[item][1]]:
                copy = describe(item, step)
                copy.start()
                sent.append(copy)
    for item in range(count):
        kind, axis = plan[item]
        if kind == "gather":
            rows = ins[item].shape[0]
            outs[item][pl.ds(pl.multiple_of(me[axis] * rows, rows), rows), :] = ins[item][...]
        elif kind == "sum":
            slots[item][me[axis]] = ins[item][...]
    for item in range(count):
        kind, axis = plan[item]
        size = sizes[axis]
        for step in range(1, size):
            arrival(item, step).wait_recv()
        if kind == "scatter":
            rows = outs[item].shape[0]
            total = ins[item][pl.ds(pl.multiple_of(me[axis] * rows, rows), rows), :].astype(jnp.float32)
            for step in range(1, size):
                origin = lax.rem(me[axis] + size - step, size)
                total = total + slots[item][origin].astype(jnp.float32)
            outs[item][...] = total
        elif kind == "sum":
            total = slots[item][0].astype(jnp.float32)
            for index in range(1, size):
                total = total + slots[item][index].astype(jnp.float32)
            outs[item][...] = total
    for copy in sent:
        copy.wait_send()


def exchange(identity, *items):
    sizes = {axis: lax.axis_size(axis) for _, axis, _ in items}
    plan, shapes, slots = [], [], []
    for kind, axis, array in items:
        size = sizes[axis]
        rows, columns = array.shape
        plan.append((kind, axis))
        if kind == "gather":
            shapes.append(jax.ShapeDtypeStruct((size * rows, columns), array.dtype))
            slots.append(pltpu.VMEM((1, 16, 128), array.dtype))
        elif kind == "scatter":
            shapes.append(jax.ShapeDtypeStruct((rows // size, columns), jnp.float32))
            slots.append(pltpu.VMEM((size, rows // size, columns), array.dtype))
        else:
            shapes.append(jax.ShapeDtypeStruct((rows, columns), jnp.float32))
            slots.append(pltpu.VMEM((size, rows, columns), array.dtype))
    most = max(sizes.values())
    return pl.pallas_call(
        partial(exchange_kernel, tuple(plan), sizes),
        out_shape=tuple(shapes),
        in_specs=[pl.BlockSpec(memory_space=pltpu.VMEM)] * len(items),
        out_specs=tuple([pl.BlockSpec(memory_space=pltpu.VMEM)] * len(items)),
        scratch_shapes=slots
        + [
            pltpu.SemaphoreType.DMA((len(items), most)),
            pltpu.SemaphoreType.DMA((len(items), most)),
        ],
        compiler_params=pltpu.CompilerParams(
            collective_id=identity, has_side_effects=True, vmem_limit_bytes=24 * 2**20
        ),
    )(*[array for _, _, array in items])


def contract_rows(left_side, right_side):
    return lax.dot_general(
        left_side, right_side, (((0,), (0,)), ((), ())), preferred_element_type=jnp.float32
    )


def times_transposed(left_side, right_side):
    return lax.dot_general(
        left_side, right_side, (((1,), (1,)), ((), ())), preferred_element_type=jnp.float32
    )


def project(normed, weight):
    return jnp.dot(normed, weight, preferred_element_type=jnp.float32)


def on_device(
    layer_input,
    lengths,
    input_gain,
    proj_gate,
    proj_values,
    proj_state,
    proj_step,
    conv_values,
    bias_values,
    conv_state,
    bias_state,
    step_bias,
    decay_log,
    skip_gain,
    mixer_gain,
    proj_output,
    out_grad,
):
    local_rows = layer_input.shape[0]
    rows_in = layer_input.astype(jnp.float32)
    inv_rms = lax.rsqrt(jnp.mean(rows_in * rows_in, axis=1, keepdims=True) + epsilon)
    normed_rows = (rows_in * inv_rms * input_gain).astype(jnp.bfloat16)
    state_columns = proj_state.shape[1]
    head_count = proj_step.shape[1]
    tail = -(state_columns + head_count) % 128
    small_w = jnp.concatenate(
        [proj_state, proj_step, jnp.zeros((proj_step.shape[0], tail), jnp.bfloat16)], axis=1
    )
    normed, gate_w, values_w, output_w, small_w = exchange(
        0,
        ("gather", "tensor", normed_rows),
        ("gather", "dp", proj_gate),
        ("gather", "dp", proj_values),
        ("gather", "dp", proj_output),
        ("gather", "dp", small_w),
    )
    state_w = small_w[:, :state_columns]
    step_w = small_w[:, state_columns : state_columns + head_count]
    upstream = lax.all_gather(out_grad, "tensor", axis=0, tiled=True)
    gate_in = project(normed, gate_w)
    values_in = project(normed, values_w)
    state_in = project(normed, state_w)
    step_in = project(normed, step_w)
    present = (jnp.arange(normed.shape[0]) < lengths[0]).astype(jnp.float32)
    (values, maps, step_sizes, cum), before_pull = jax.vjp(
        partial(before_scan, present=present),
        values_in,
        state_in,
        step_in,
        conv_values,
        bias_values,
        conv_state,
        bias_state,
        step_bias,
        decay_log,
    )
    low_values, low_maps = values.astype(jnp.bfloat16), maps.astype(jnp.bfloat16)
    scanned, kept = scan_forward(low_values, low_maps, step_sizes, cum)
    gated, after_pull = jax.vjp(
        partial(after_scan, present=present), scanned, values, gate_in, skip_gain
    )
    grad_normed_out = jnp.dot(upstream, output_w, preferred_element_type=jnp.float32)
    scaled_grad = grad_normed_out * mixer_gain
    row_sums = jnp.stack([jnp.sum(gated * gated, axis=1), jnp.sum(scaled_grad * gated, axis=1)])
    (row_sums,) = exchange(
        1, ("sum", "tensor", jnp.pad(row_sums, ((0, 6), (0, 0))))
    )
    inv_norm = lax.rsqrt(row_sums[0] / INNER + epsilon)[:, None]
    cross = row_sums[1]
    normed_out = (gated * inv_norm * mixer_gain).astype(jnp.bfloat16)
    mixed_rows = lax.psum_scatter(
        times_transposed(normed_out, output_w).astype(jnp.bfloat16),
        "tensor",
        scatter_dimension=0,
        tiled=True,
    )
    layer_output = (rows_in + mixed_rows.astype(jnp.float32)).astype(jnp.bfloat16)
    grad_output_w = contract_rows(upstream, normed_out)
    grad_mixer_gain = jnp.sum(grad_normed_out * gated * inv_norm, axis=0)
    grad_gated = (
        inv_norm * scaled_grad - gated * (inv_norm * inv_norm * inv_norm) * (cross / INNER)[:, None]
    )
    grad_scanned, grad_values, grad_gate_in, grad_skip_gain = after_pull(grad_gated)
    scan_values, grad_maps, grad_step, grad_cum = scan_backward(
        low_values, low_maps, step_sizes, cum, kept, grad_scanned
    )
    (
        grad_values_in,
        grad_state_part,
        grad_step_in,
        grad_conv_values,
        grad_bias_values,
        grad_conv_part,
        grad_shift_part,
        grad_step_bias,
        grad_decay_log,
    ) = before_pull((grad_values + scan_values, grad_maps, grad_step, grad_cum))
    own_state, owned_output = exchange(
        2,
        ("scatter", "tensor", grad_state_part.astype(jnp.bfloat16)),
        ("scatter", "dp", grad_output_w.astype(jnp.bfloat16)),
    )
    own_state = own_state.astype(jnp.bfloat16)
    low_gate = grad_gate_in.astype(jnp.bfloat16)
    low_values = grad_values_in.astype(jnp.bfloat16)
    low_step = grad_step_in.astype(jnp.bfloat16)
    grad_gate_w = contract_rows(normed, low_gate)
    grad_values_w = contract_rows(normed, low_values)
    grad_small_w = jnp.concatenate(
        [
            contract_rows(normed_rows, own_state),
            contract_rows(normed, low_step),
            jnp.zeros((normed.shape[1], tail), jnp.float32),
        ],
        axis=1,
    )
    summed = times_transposed(low_gate, gate_w)
    summed = summed + times_transposed(low_values, values_w)
    head_part = summed + times_transposed(low_step, step_w)
    head_part, owned_gate, owned_values, owned_small = exchange(
        3,
        ("scatter", "tensor", head_part.astype(jnp.bfloat16)),
        ("scatter", "dp", grad_gate_w.astype(jnp.bfloat16)),
        ("scatter", "dp", grad_values_w.astype(jnp.bfloat16)),
        ("scatter", "dp", grad_small_w.astype(jnp.bfloat16)),
    )
    grad_normed_rows = head_part + times_transposed(own_state, state_w)
    scaled_in = grad_normed_rows * input_gain
    cross_in = jnp.mean(scaled_in * rows_in, axis=1, keepdims=True)
    input_grad = (
        out_grad.astype(jnp.float32)
        + inv_rms * scaled_in
        - rows_in * (inv_rms * inv_rms * inv_rms) * cross_in
    ).astype(jnp.bfloat16)
    grad_gain_part = jnp.sum(grad_normed_rows * rows_in * inv_rms, axis=0)
    width = grad_gain_part.shape[0]
    channels = grad_bias_values.shape[0]

    def packed(parts, columns):
        flat = jnp.concatenate([part.reshape(-1) for part in parts])
        filled = -(-flat.shape[0] // (8 * columns)) * 8 * columns
        return jnp.pad(flat, (0, filled - flat.shape[0])).reshape(-1, columns)

    def unpacked(table, parts):
        flat, start, out = table.reshape(-1), 0, []
        for part in parts:
            out.append(flat[start : start + part.size].reshape(part.shape))
            start += part.size
        return out

    shared = [grad_gain_part, grad_conv_part, grad_shift_part]
    shared_sum, owned_state = exchange(
        4,
        ("sum", "tensor", packed(shared, width)),
        ("sum", "tensor", owned_small[:, :state_columns].astype(jnp.bfloat16)),
    )
    own = [
        grad_conv_values,
        grad_bias_values,
        grad_mixer_gain,
        grad_step_bias,
        grad_decay_log,
        grad_skip_gain,
    ]
    shared_sum, own_sum = exchange(
        5,
        ("sum", "dp", shared_sum),
        ("sum", "dp", packed(own, channels)),
    )
    grad_gain, grad_conv_state, grad_bias_state = unpacked(shared_sum, shared)
    (
        grad_conv_values,
        grad_bias_values,
        grad_mixer_gain,
        grad_step_bias,
        grad_decay_log,
        grad_skip_gain,
    ) = unpacked(own_sum, own)
    return (
        layer_output,
        input_grad,
        grad_gain,
        owned_gate,
        owned_values,
        owned_state,
        owned_small[:, state_columns : state_columns + head_count],
        grad_conv_values,
        grad_bias_values,
        grad_conv_state,
        grad_bias_state,
        grad_step_bias,
        grad_decay_log,
        grad_skip_gain,
        grad_mixer_gain,
        owned_output,
    )


def solution(mesh):
    return jax.shard_map(
        on_device,
        mesh=mesh,
        in_specs=(
            P(("dp", "tensor"), None),
            P("dp"),
            P(),
            P("dp", "tensor"),
            P("dp", "tensor"),
            P("dp", None),
            P("dp", "tensor"),
            P(None, "tensor"),
            P("tensor"),
            P(),
            P(),
            P("tensor"),
            P("tensor"),
            P("tensor"),
            P("tensor"),
            P("dp", "tensor"),
            P(("dp", "tensor"), None),
        ),
        out_specs=(
            P(("dp", "tensor"), None),
            P(("dp", "tensor"), None),
            P(),
            P("dp", "tensor"),
            P("dp", "tensor"),
            P("dp", None),
            P("dp", "tensor"),
            P(None, "tensor"),
            P("tensor"),
            P(),
            P(),
            P("tensor"),
            P("tensor"),
            P("tensor"),
            P("tensor"),
            P("dp", "tensor"),
        ),
        check_vma=False,
    )
```
